32 devices in a mesh: dp: 2 (over x), tp: 4 (over y, core), fsdp: 4 (over z).
Axes of the slice: x: 2, y: 2, z: 4, core: 2. Of those that a mesh axis runs over, the one named last changes fastest.
Arguments:
- hidden: bfloat16 [8, 2, 128, 2432], P(('dp', 'fsdp')), may hold values from -6 to 6
- text_kv: bfloat16 [8, 2, 333, 24, 128], P(('dp', 'fsdp'), None, None, 'tp'), may hold values from -6 to 6
- mods: bfloat16 [8, 2, 5, 2432], P(('dp', 'fsdp')), may hold values from -5 to 5
- latents: float32 [8, 128, 64], P(('dp', 'fsdp')), may hold values from -6 to 6
- noise: float32 [8, 128, 64], P(('dp', 'fsdp')), may hold values from -6 to 6
- step_index: int32 [8], P(('dp', 'fsdp')), may hold values from 1 to 8
- group_id: int32 [8], P(('dp', 'fsdp')), may hold values from 0 to 3
- advantages: float32 [8], P(('dp', 'fsdp')), may hold values from -4 to 4
- w_qkv: bfloat16 [2432, 3, 1536], P(('dp', 'fsdp'), None, 'tp'), may hold values from -0.125 to 0.125
- w_out: bfloat16 [2432, 1536], P(('dp', 'fsdp'), 'tp'), may hold values from -0.15625 to 0.15625
- w_final: bfloat16 [2432, 64], P(('dp', 'fsdp')), may hold values from -0.125 to 0.125
Outputs:
- next_latents: float32 [8, 128, 64], P(('dp', 'fsdp'))
- log_prob: float32 [8], P(('dp', 'fsdp'))
- grad_out: float32 [2432, 1536], P(('dp', 'fsdp'), 'tp')
- grad_final: float32 [2432, 64], P(('dp', 'fsdp'))
The draws below stay inside these ranges and needn't reach their ends.
All inputs are finite; a program needn't handle non-finite values.
Results may differ from the reference program's by a relative error of at most 0.006.
Values may be sent and summed in bfloat16 or wider, within the bound.
A program may use at most 64 MiB of HBM per device.

```python
import math
import jax
import jax.numpy as jnp
from jax import lax

D = 2432
HEAD = 64
HEADS = 24
IMG = 128
TXT = 333
PATCH = 64
STEPS = 10
GROUPS = 4
SAMPLES = 8


def with_ends(values, stream_key, low, largest):
    longest = values.shape.index(max(values.shape))
    spots = []
    for shift in (0, 1):
        where = [jax.random.randint(jax.random.fold_in(stream_key, axis), (), 0, length) for axis, length in enumerate(values.shape)]
        where[longest] = (where[longest] + shift) % values.shape[longest]
        spots.append(tuple(where))
    return values.at[spots[0]].set(low).at[spots[1]].set(largest)


def block_scale(stream_key, shape, pieces, smallest, high):
    def one(position, blocks):
        draws = jax.random.uniform(jax.random.fold_in(jax.random.fold_in(stream_key, 6), position), (blocks,), jnp.float32, smallest / len(pieces), high / len(pieces))
        return jnp.repeat(jnp.exp(draws), shape[position] // blocks).reshape((-1,) + (1,) * (len(shape) - position - 1))

    factor_of = one(*pieces[0])
    for cut in pieces[1:]:
        factor_of = factor_of * one(*cut)
    return factor_of


def scatter_about(own_key, extent, scale, bound, shards=(), held_as=jnp.bfloat16):
    entries = scale * jax.random.normal(own_key, extent, jnp.float32)
    if shards:
        entries = entries * block_scale(own_key, extent, shards, -0.22, 0.18)
    return jnp.clip(entries, -bound, bound).astype(held_as)


def setup_inputs(seed: int = 0) -> dict:
    key_of = jax.random.split(jax.random.key(seed), 12)
    return {
        "hidden": scatter_about(key_of[0], (SAMPLES, 2, IMG, D), 1.0, 6.0, ((0, 8),)),
        "text_kv": scatter_about(key_of[1], (SAMPLES, 2, TXT, HEADS, 2 * HEAD), 1.0, 6.0, ((0, 8), (3, 4))),
        "mods": scatter_about(key_of[2], (SAMPLES, 2, 5, D), 0.8, 5.0, ((0, 8),)),
        "latents": scatter_about(key_of[3], (SAMPLES, IMG, PATCH), 1.0, 6.0, ((0, 8),), jnp.float32),
        "noise": scatter_about(key_of[4], (SAMPLES, IMG, PATCH), 1.0, 6.0, ((0, 8),), jnp.float32),
        "step_index": with_ends(jax.random.randint(key_of[5], (SAMPLES,), 1, STEPS - 1), jax.random.fold_in(key_of[5], 1), 1, (STEPS - 1) - 1).astype(jnp.int32),
        "group_id": with_ends(jax.random.randint(key_of[6], (SAMPLES,), 0, GROUPS), jax.random.fold_in(key_of[6], 1), 0, GROUPS - 1).astype(jnp.int32),
        "advantages": scatter_about(key_of[7], (SAMPLES,), 1.0, 4.0, ((0, 8),), jnp.float32),
        "w_qkv": scatter_about(key_of[8], (D, 3, HEADS * HEAD), D ** -0.5, 0.125, ((0, 8), (2, 4))),
        "w_out": scatter_about(key_of[9], (D, HEADS * HEAD), (HEADS * HEAD) ** -0.5, 0.15625, ((0, 8), (1, 4))),
        "w_final": scatter_about(key_of[10], (D, PATCH), D ** -0.5, 0.125, ((0, 8),)),
    }


eps_norm = 1e-06
time_shift = 3.0
noise_level = 0.7
guidance = 4.5
loss_scale = 2048.0

def layer_norm(values):
    centred = values - lax.optimization_barrier(jnp.mean(values, axis=-1, keepdims=True))
    inverse = lax.rsqrt(lax.optimization_barrier(jnp.mean(centred * centred, axis=-1, keepdims=True)) + eps_norm)
    return (centred * inverse, inverse)

def layer_norm_back(upstream, normed, inverse):
    return inverse * (upstream - lax.optimization_barrier(jnp.mean(upstream, axis=-1, keepdims=True)) - normed * lax.optimization_barrier(jnp.mean(upstream * normed, axis=-1, keepdims=True)))

def rms_norm(values):
    inverse = lax.rsqrt(lax.optimization_barrier(jnp.mean(values * values, axis=-1, keepdims=True)) + eps_norm)
    return values * inverse

def plan(sample_step, step_count):
    level_now = 1.0 - sample_step.astype(jnp.float32) / step_count
    level_next = 1.0 - (sample_step + 1).astype(jnp.float32) / step_count
    time_now = time_shift * level_now / (1.0 + (time_shift - 1.0) * level_now)
    time_next = time_shift * level_next / (1.0 + (time_shift - 1.0) * level_next)
    noise_scale = noise_level * jnp.sqrt(time_now / (1.0 - time_now))
    return (time_now, time_now - time_next, noise_scale)

def transition(latent, noise_draw, velocity, sample_step, step_count):
    time_now, step_size, noise_scale = plan(sample_step, step_count)
    spread = noise_scale * jnp.sqrt(step_size)
    drift_velocity = 1.0 + noise_scale * noise_scale * (1.0 - time_now) / (2.0 * time_now)
    drift_latent = noise_scale * noise_scale / (2.0 * time_now)
    centre = latent - step_size * (drift_velocity * velocity + drift_latent * latent)
    following = centre + spread * noise_draw
    offset = following - centre
    log_density = jnp.mean(-offset * offset / (2.0 * spread * spread) - jnp.log(spread) - 0.5 * math.log(2.0 * math.pi))
    slope = step_size * drift_velocity * offset / (spread * spread * offset.size)
    return (following, log_density, slope)

def attend(projected, text_pair):
    head_width = projected.shape[-1]
    query = rms_norm(projected[:, 0])
    key_image = rms_norm(projected[:, 1])
    key_text = rms_norm(text_pair[..., :head_width].astype(jnp.float32))
    query_half = query.astype(jnp.bfloat16)
    key_all = jnp.concatenate([key_image.astype(jnp.bfloat16), key_text.astype(jnp.bfloat16)], 0)
    value_all = jnp.concatenate([projected[:, 2].astype(jnp.bfloat16), text_pair[..., head_width:]], 0)
    score_scale = 1.0 / math.sqrt(head_width)
    scores = jnp.einsum('qhe,khe->hqk', query_half.astype(jnp.float32), key_all.astype(jnp.float32)) * score_scale
    exponent = jnp.exp(scores)
    attention = exponent / lax.optimization_barrier(jnp.sum(exponent, axis=-1, keepdims=True))
    attention_half = attention.astype(jnp.bfloat16)
    return jnp.einsum('hqk,khe->qhe', attention_half.astype(jnp.float32), value_all.astype(jnp.float32)).astype(jnp.bfloat16)

def reference(hidden, text_kv, mods, latents, noise, step_index, group_id, advantages, w_qkv, w_out, w_final):
    onehot = (group_id[:, None] == jnp.arange(GROUPS, dtype=jnp.int32)[None, :]).astype(jnp.float32)
    counts = lax.optimization_barrier(jnp.sum(onehot, axis=0))
    members = lax.optimization_barrier(jnp.sum(onehot * counts[None, :], axis=1))
    sample_weights = loss_scale * advantages / members
    model_width = hidden.shape[-1]
    flat_qkv = w_qkv.reshape(model_width, -1)

    def per_sample(carry, inputs):
        hidden_pair, text_pair, modulation, latent, noise_draw, sample_step, sample_weight = inputs
        row_count = hidden_pair.shape[1]
        heads = text_pair.shape[2]
        residual = hidden_pair.astype(jnp.float32)
        mod_values = modulation.astype(jnp.float32)
        normed, inverse = layer_norm(residual)
        modulated = (normed * (1.0 + mod_values[:, 1:2]) + mod_values[:, 0:1]).astype(jnp.bfloat16)
        records = []
        velocities = []
        for which in range(2):
            projected = jnp.dot(modulated[which], flat_qkv, preferred_element_type=jnp.float32).reshape(row_count, 3, heads, -1)
            attended = attend(projected, text_pair[which])
            attended_flat = attended.reshape(row_count, -1)
            partial_sum = jnp.dot(attended_flat, w_out.T, preferred_element_type=jnp.float32)
            updated = residual[which] + mod_values[which, 2] * partial_sum
            final_normed, final_inverse = layer_norm(updated)
            readout = (final_normed * (1.0 + mod_values[which, 4]) + mod_values[which, 3]).astype(jnp.bfloat16)
            velocities.append(jnp.dot(readout, w_final, preferred_element_type=jnp.float32))
            records.append((attended_flat, final_normed, final_inverse, readout))
        guided = velocities[1] + guidance * (velocities[0] - velocities[1])
        following, log_density, slope = transition(latent, noise_draw, guided, sample_step, STEPS)
        upstream_velocity = sample_weight * slope
        grad_out, grad_final = carry
        for which, factor in ((0, guidance), (1, 1.0 - guidance)):
            attended_flat, final_normed, final_inverse, readout = records[which]
            velocity_grad = (factor * upstream_velocity).astype(jnp.bfloat16)
            readout_grad = jnp.dot(velocity_grad, w_final.T, preferred_element_type=jnp.float32)
            grad_final = grad_final + jnp.dot(readout.T, velocity_grad, preferred_element_type=jnp.float32)
            updated_grad = layer_norm_back(readout_grad * (1.0 + mod_values[which, 4]), final_normed, final_inverse)
            partial_grad = (mod_values[which, 2] * updated_grad).astype(jnp.bfloat16)
            grad_out = grad_out + jnp.dot(partial_grad.T, attended_flat, preferred_element_type=jnp.float32)
        return ((grad_out, grad_final), (following, log_density))
    start = (jnp.zeros(w_out.shape, jnp.float32), jnp.zeros(w_final.shape, jnp.float32))
    carry, outputs = lax.scan(per_sample, start, (hidden, text_kv, mods, latents, noise, step_index, sample_weights))
    return (outputs[0], outputs[1], carry[0], carry[1])
```

```python
import functools
import math

import jax
import jax.numpy as jnp
from jax import lax
from jax.experimental import pallas as pl
from jax.experimental.pallas import tpu as pltpu
from jax.sharding import PartitionSpec as P

STEPS = 10
GROUPS = 4
ROW_FIRST = (3, 4)


eps_norm = 1e-06
time_shift = 3.0
noise_level = 0.7
guidance = 4.5
loss_scale = 2048.0


def layer_norm(values):
    centred = values - jnp.mean(values, axis=-1, keepdims=True)
    inverse = lax.rsqrt(jnp.mean(centred * centred, axis=-1, keepdims=True) + eps_norm)
    return (centred * inverse, inverse)


def layer_norm_back(upstream, normed, inverse):
    return inverse * (
        upstream
        - jnp.mean(upstream, axis=-1, keepdims=True)
        - normed * jnp.mean(upstream * normed, axis=-1, keepdims=True)
    )


def rms_norm(values):
    inverse = lax.rsqrt(jnp.mean(values * values, axis=-1, keepdims=True) + eps_norm)
    return values * inverse


def plan(sample_step, step_count):
    level_now = 1.0 - sample_step.astype(jnp.float32) / step_count
    level_next = 1.0 - (sample_step + 1).astype(jnp.float32) / step_count
    time_now = time_shift * level_now / (1.0 + (time_shift - 1.0) * level_now)
    time_next = time_shift * level_next / (1.0 + (time_shift - 1.0) * level_next)
    noise_scale = noise_level * jnp.sqrt(time_now / (1.0 - time_now))
    return (time_now, time_now - time_next, noise_scale)


def transition(latent, noise_draw, velocity, sample_step, step_count):
    time_now, step_size, noise_scale = plan(sample_step, step_count)
    spread = noise_scale * jnp.sqrt(step_size)
    drift_velocity = 1.0 + noise_scale * noise_scale * (1.0 - time_now) / (2.0 * time_now)
    drift_latent = noise_scale * noise_scale / (2.0 * time_now)
    centre = latent - step_size * (drift_velocity * velocity + drift_latent * latent)
    following = centre + spread * noise_draw
    offset = following - centre
    log_density = jnp.mean(
        -offset * offset / (2.0 * spread * spread) - jnp.log(spread) - 0.5 * math.log(2.0 * math.pi)
    )
    slope = step_size * drift_velocity * offset / (spread * spread * offset.size)
    return (following, log_density, slope)


def attend(projected, text_pair):
    head_width = projected.shape[-1]
    query = rms_norm(projected[:, :, 0])
    key_image = rms_norm(projected[:, :, 1])
    key_text = rms_norm(text_pair[..., :head_width].astype(jnp.float32))
    query_half = query.astype(jnp.bfloat16)
    key_all = jnp.concatenate([key_image.astype(jnp.bfloat16), key_text.astype(jnp.bfloat16)], 1)
    value_all = jnp.concatenate(
        [projected[:, :, 2].astype(jnp.bfloat16), text_pair[..., head_width:]], 1
    )
    score_scale = 1.0 / math.sqrt(head_width)
    scores = (
        jnp.einsum("bqhe,bkhe->bhqk", query_half, key_all, preferred_element_type=jnp.float32)
        * score_scale
    )
    exponent = jnp.exp(scores)
    attention = exponent / jnp.sum(exponent, axis=-1, keepdims=True)
    attention_half = attention.astype(jnp.bfloat16)
    return jnp.einsum(
        "bhqk,bkhe->bqhe", attention_half, value_all, preferred_element_type=jnp.float32
    ).astype(jnp.bfloat16)


def greet(peers):
    barrier = pltpu.get_barrier_semaphore()
    for there, peer in peers:
        @pl.when(there)
        def _():
            pl.semaphore_signal(
                barrier, inc=1, device_id=peer, device_id_type=pl.DeviceIdType.MESH
            )
    pl.semaphore_wait(barrier, sum(jnp.where(there, 1, 0) for there, _ in peers))


def remote(src, dst, send_sem, recv_sem, peer):
    return pltpu.make_async_remote_copy(
        src_ref=src,
        dst_ref=dst,
        send_sem=send_sem,
        recv_sem=recv_sem,
        device_id=peer,
        device_id_type=pl.DeviceIdType.MESH,
    )


def around(dp_size, line_size):
    row, spot = lax.axis_index("dp"), lax.axis_index("fsdp")
    across = [{"dp": lax.rem(row + k, dp_size)} for k in range(1, dp_size)]
    right, left = {"fsdp": lax.rem(spot + 1, line_size)}, {
        "fsdp": lax.rem(spot + line_size - 1, line_size)
    }
    has_right, has_left = spot < line_size - 1, spot > 0
    peers = [(row >= 0, peer) for peer in across] + [(has_right, right), (has_left, left)]
    return row, spot, across, (right, left), (has_right, has_left), peers


def gather_kernel(
    dp_size, line_size, row_first, blocks_ref, thin_ref, all_ref, all_thin_ref,
    local_sem, recv_sem, line_sem, across_sem,
):
    row, spot, across, sides, has_side, peers = around(dp_size, line_size)
    count = blocks_ref.shape[0]
    me = row * line_size + spot

    def mine(k):
        return blocks_ref.at[k] if k < count else thin_ref

    def slot(k, which):
        return all_ref.at[k, which] if k < count else all_thin_ref.at[which]

    def along(k, which, side, own):
        src = mine(k) if own else slot(k, which)
        return remote(
            src, slot(k, which), line_sem.at[side, k, which], recv_sem.at[k, which], sides[side]
        )

    def over(k, stop, hop, own):
        which = row * line_size + stop
        src = mine(k) if own else slot(k, which)
        return remote(
            src, slot(k, which), across_sem.at[hop, k, stop], recv_sem.at[k, which], across[hop]
        )

    def arrived(k, which):
        along(k, which, 0, False).wait_recv()

    def when(condition, action):
        @pl.when(condition)
        def _():
            action()

    order = list(range(count + 1))
    greet(peers)
    keep = [pltpu.make_async_copy(mine(k), slot(k, me), local_sem.at[k]) for k in order]
    started = []

    def go(condition, copy):
        when(condition, lambda: copy.start())
        started.append((condition, copy))

    always = row >= 0

    def own_sends(k):
        for side in (0, 1):
            go(has_side[side], along(k, me, side, True))
        for hop in range(dp_size - 1):
            go(always, over(k, spot, hop, True))

    first = [k for k in order if k in row_first]
    rest = [k for k in order if k not in row_first]
    for k in rest:
        own_sends(k)
    for copy in keep:
        copy.start()

    def pass_on(k, step, hop):
        from_row = row if hop is None else lax.rem(row + dp_size - hop - 1, dp_size)
        for side in (0, 1):
            stop = spot - step if side == 0 else spot + step
            there = stop >= 0 if side == 0 else stop < line_size
            safe = lax.rem(stop + line_size, line_size)
            which = from_row * line_size + safe
            when(there, functools.partial(arrived, k, which))
            go(there & has_side[side], along(k, which, side, False))
            if k not in row_first:
                for other in range(dp_size - 1):
                    go(there, over(k, safe, other, False))

    def row_arrivals(k):
        for hop in range(dp_size - 1):
            which = lax.rem(row + dp_size - hop - 1, dp_size) * line_size + spot
            arrived(k, which)
            if k in row_first:
                for side in (0, 1):
                    go(has_side[side], along(k, which, side, False))

    for step in range(1, line_size):
        for k in rest:
            pass_on(k, step, None)
        if step == 1:
            for k in first:
                own_sends(k)
    for k in first:
        row_arrivals(k)
    for step in range(1, line_size):
        for k in first:
            for hop in [None] + list(range(dp_size - 1)):
                pass_on(k, step, hop)
    for k in rest:
        for stop in range(line_size):
            for hop in range(dp_size - 1):
                arrived(k, lax.rem(row + dp_size - hop - 1, dp_size) * line_size + stop)
    for copy in keep:
        copy.wait()
    for condition, copy in started:
        when(condition, functools.partial(copy.wait_send))


def gather_rows(blocks, thin, dp_size, line_size):
    kinds = blocks.shape[0] + 1
    total = dp_size * line_size
    dma = pltpu.SemaphoreType.DMA
    return pl.pallas_call(
        functools.partial(gather_kernel, dp_size, line_size, ROW_FIRST),
        out_shape=(
            jax.ShapeDtypeStruct((blocks.shape[0], total) + blocks.shape[1:], blocks.dtype),
            jax.ShapeDtypeStruct((total,) + thin.shape, thin.dtype),
        ),
        in_specs=[pl.BlockSpec(memory_space=pl.ANY)] * 2,
        out_specs=(pl.BlockSpec(memory_space=pl.ANY),) * 2,
        scratch_shapes=[
            dma((kinds,)),
            dma((kinds, total)),
            dma((2, kinds, total)),
            dma((max(dp_size - 1, 1), kinds, line_size)),
        ],
        compiler_params=pltpu.CompilerParams(collective_id=0, has_side_effects=True),
    )(blocks, thin)


def scatter_kernel(
    dp_size, line_size, part_ref, out_ref, row_in, line_in, line_out,
    row_send, row_recv, line_send, line_recv,
):
    row, spot, across, sides, has_side, peers = around(dp_size, line_size)

    def over(stop, hop):
        target = lax.rem(row + hop + 1, dp_size) * line_size + stop
        return remote(
            part_ref.at[target], row_in.at[hop, stop], row_send.at[hop, stop],
            row_recv.at[hop, stop], across[hop],
        )

    def along(stop, side):
        return remote(
            line_out.at[stop], line_in.at[side, stop], line_send.at[stop],
            line_recv.at[side, stop], sides[side],
        )

    def row_sum(stop):
        value = part_ref[row * line_size + stop].astype(jnp.float32)
        for hop in range(dp_size - 1):
            over(stop, hop).wait_recv()
            value = value + row_in[hop, stop].astype(jnp.float32)
        return value

    def launch(stop):
        for hop in range(dp_size - 1):
            over(stop, hop).start()

    def step(stop, side):
        from_side = has_side[1 - side]
        line_out[stop] = row_sum(stop).astype(line_out.dtype)

        @pl.when(from_side)
        def _():
            along(stop, side).wait_recv()
            line_out[stop] = (
                line_out[stop].astype(jnp.float32) + line_in[side, stop].astype(jnp.float32)
            ).astype(line_out.dtype)

        along(stop, side).start()

    greet(peers)
    turns = []
    for turn in range(line_size - 1):
        turns.append((line_size - 1 - turn, 0))
        turns.append((turn, 1))
    for stop, side in turns:
        @pl.when(stop > spot if side == 0 else stop < spot)
        def _():
            launch(stop)
    launch(spot)
    for stop, side in turns:
        @pl.when(stop > spot if side == 0 else stop < spot)
        def _():
            step(stop, side)
    out_ref[...] = row_sum(spot)
    for side in (0, 1):
        @pl.when(has_side[1 - side])
        def _():
            along(spot, side).wait_recv()
            out_ref[...] = out_ref[...] + line_in[side, spot].astype(jnp.float32)
    for stop in range(line_size):
        for hop in range(dp_size - 1):
            over(stop, hop).wait_send()
    for stop, side in turns:
        @pl.when(stop > spot if side == 0 else stop < spot)
        def _():
            along(stop, side).wait_send()


def scatter_rows(parts, dp_size, line_size):
    block = parts.shape[1:]
    hops = max(dp_size - 1, 1)
    dma = pltpu.SemaphoreType.DMA
    return pl.pallas_call(
        functools.partial(scatter_kernel, dp_size, line_size),
        out_shape=jax.ShapeDtypeStruct(block, jnp.float32),
        in_specs=[pl.BlockSpec(memory_space=pltpu.VMEM)],
        out_specs=pl.BlockSpec(memory_space=pltpu.VMEM),
        scratch_shapes=[
            pltpu.VMEM((hops, line_size) + block, jnp.bfloat16),
            pltpu.VMEM((2, line_size) + block, jnp.bfloat16),
            pltpu.VMEM((line_size,) + block, jnp.bfloat16),
            dma((hops, line_size)),
            dma((hops, line_size)),
            dma((line_size,)),
            dma((2, line_size)),
        ],
        compiler_params=pltpu.CompilerParams(
            collective_id=1, has_side_effects=True, vmem_limit_bytes=48 * 1024 * 1024
        ),
    )(parts)


def heads_kernel(
    attended_ref, rows_ref, out_ref, total, out_first, in_first, out_second, in_second,
    send_sem, recv_sem,
):
    me = lax.axis_index("tp")
    low, high = lax.rem(me, 2), me // 2
    near, far = {"tp": me + 1 - 2 * low}, {"tp": lax.rem(me + 2, 4)}
    greet([(me >= 0, near), (me >= 0, far)])

    def product(which):
        return lax.dot_general(
            attended_ref[which], rows_ref[...], (((1,), (1,)), ((), ())),
            preferred_element_type=jnp.float32,
        )

    half = total.shape[1]
    out_first[...] = product(1 - low).astype(jnp.bfloat16)
    first = remote(out_first, in_first, send_sem.at[0], recv_sem.at[0], near)
    first.start()
    total[...] = product(low).reshape(total.shape)
    first.wait_recv()
    total[...] = total[...] + in_first[...].reshape(total.shape).astype(jnp.float32)
    out_second[...] = total[1 - high].astype(jnp.bfloat16)
    second = remote(out_second, in_second, send_sem.at[1], recv_sem.at[1], far)
    second.start()
    second.wait_recv()
    out_ref[low, high] = (total[high] + in_second[...].astype(jnp.float32)).astype(jnp.bfloat16)
    done = out_ref.at[low, high]
    third = remote(done, done, send_sem.at[2], recv_sem.at[2], far)
    third.start()
    fourth = remote(done, done, send_sem.at[3], recv_sem.at[3], near)
    fourth.start()
    remote(done, out_ref.at[low, 1 - high], send_sem.at[2], recv_sem.at[2], far).wait_recv()
    other = out_ref.at[low, 1 - high]
    fifth = remote(other, other, send_sem.at[4], recv_sem.at[4], near)
    fifth.start()
    fourth.wait_recv()
    fifth.wait_recv()
    for copy in (first, second, third, fourth, fifth):
        copy.wait_send()


def head_sum(attended, out_rows):
    _, tokens, _ = attended.shape
    width = out_rows.shape[0]
    half = tokens // 2
    return pl.pallas_call(
        heads_kernel,
        out_shape=jax.ShapeDtypeStruct((2, 2, half, width), jnp.bfloat16),
        in_specs=[pl.BlockSpec(memory_space=pltpu.VMEM)] * 2,
        out_specs=pl.BlockSpec(memory_space=pltpu.VMEM),
        scratch_shapes=[
            pltpu.VMEM((2, half, width), jnp.float32),
            pltpu.VMEM((tokens, width), jnp.bfloat16),
            pltpu.VMEM((tokens, width), jnp.bfloat16),
            pltpu.VMEM((half, width), jnp.bfloat16),
            pltpu.VMEM((half, width), jnp.bfloat16),
            pltpu.SemaphoreType.DMA((5,)),
            pltpu.SemaphoreType.DMA((5,)),
        ],
        compiler_params=pltpu.CompilerParams(
            collective_id=2, has_side_effects=True, vmem_limit_bytes=48 * 1024 * 1024
        ),
    )(attended, out_rows).reshape(2, tokens, width)


def contract_rows(left, right):
    return lax.dot_general(
        left, right, (((0,), (0,)), ((), ())), preferred_element_type=jnp.float32
    )


def local(
    hidden, text_kv, mods, latents, noise, step_index, group_id, advantages, w_qkv, w_out, w_final
):
    row_count = hidden.shape[2]
    model_width = hidden.shape[3]
    heads = text_kv.shape[3]
    head_width = text_kv.shape[4] // 2
    head_columns = heads * head_width
    residual = hidden[0].astype(jnp.float32)
    mod_values = mods[0].astype(jnp.float32)
    normed, inverse = layer_norm(residual)
    modulated = (normed * (1.0 + mod_values[:, 1:2]) + mod_values[:, 0:1]).astype(jnp.bfloat16)
    stacked = modulated.reshape(2 * row_count, model_width)
    dp_size, line_size = lax.axis_size("dp"), lax.axis_size("fsdp")
    blocks = jnp.concatenate([jnp.swapaxes(w_qkv, 0, 1), w_out[None]], 0)
    gathered, final_rows = gather_rows(blocks, w_final, dp_size, line_size)
    gathered = gathered.reshape(4, model_width, head_columns)
    final_rows = final_rows.reshape(model_width, -1)
    out_rows = gathered[3]
    projected = jnp.stack(
        [jnp.dot(stacked, gathered[k], preferred_element_type=jnp.float32) for k in range(3)], 1
    )
    projected = projected.reshape(2, row_count, 3, heads, head_width)
    attended = attend(projected, text_kv[0])
    attended_flat = attended.reshape(2, row_count, head_columns)
    partial_sum = head_sum(attended_flat, out_rows).astype(jnp.float32)
    updated = residual + mod_values[:, 2:3] * partial_sum
    final_normed, final_inverse = layer_norm(updated)
    readout = (final_normed * (1.0 + mod_values[:, 4:5]) + mod_values[:, 3:4]).astype(jnp.bfloat16)
    velocity = jnp.einsum("brd,dp->brp", readout, final_rows, preferred_element_type=jnp.float32)
    guided = velocity[1] + guidance * (velocity[0] - velocity[1])
    following, log_density, slope = transition(latents[0], noise[0], guided, step_index[0], STEPS)
    onehot = (group_id[0] == jnp.arange(GROUPS, dtype=jnp.int32)).astype(jnp.float32)
    counts = lax.psum(onehot, ("dp", "fsdp"))
    members = jnp.sum(onehot * counts)
    sample_weight = loss_scale * advantages[0] / members
    upstream_velocity = sample_weight * slope
    velocity_grad = jnp.stack(
        [guidance * upstream_velocity, (1.0 - guidance) * upstream_velocity], 0
    ).astype(jnp.bfloat16)
    readout_grad = jnp.einsum(
        "brp,dp->brd", velocity_grad, final_rows, preferred_element_type=jnp.float32
    )
    updated_grad = layer_norm_back(
        readout_grad * (1.0 + mod_values[:, 4:5]), final_normed, final_inverse
    )
    partial_grad = (mod_values[:, 2:3] * updated_grad).astype(jnp.bfloat16)
    readout_flat = readout.reshape(2 * row_count, model_width)
    velocity_flat = velocity_grad.reshape(2 * row_count, -1)
    partial_flat = partial_grad.reshape(2 * row_count, model_width)
    attended_rows = attended_flat.reshape(2 * row_count, head_columns)
    parts = jnp.concatenate(
        [
            contract_rows(partial_flat, attended_rows).astype(jnp.bfloat16),
            contract_rows(readout_flat, velocity_flat).astype(jnp.bfloat16),
        ],
        1,
    )
    sums = scatter_rows(
        parts.reshape(dp_size * line_size, -1, parts.shape[1]), dp_size, line_size
    )
    grad_out, grad_final = sums[:, :head_columns], sums[:, head_columns:]
    return (following[None], log_density[None], grad_out, grad_final)


def solution(mesh):
    in_specs = (
        P(("dp", "fsdp"), None, None, None),
        P(("dp", "fsdp"), None, None, "tp", None),
        P(("dp", "fsdp"), None, None, None),
        P(("dp", "fsdp"), None, None),
        P(("dp", "fsdp"), None, None),
        P(("dp", "fsdp")),
        P(("dp", "fsdp")),
        P(("dp", "fsdp")),
        P(("dp", "fsdp"), None, "tp"),
        P(("dp", "fsdp"), "tp"),
        P(("dp", "fsdp"), None),
    )
    out_specs = (
        P(("dp", "fsdp"), None, None),
        P(("dp", "fsdp")),
        P(("dp", "fsdp"), "tp"),
        P(("dp", "fsdp"), None),
    )
    return jax.shard_map(local, mesh=mesh, in_specs=in_specs, out_specs=out_specs, check_vma=False)
```

```python
import functools
import math

import jax
import jax.numpy as jnp
from jax import lax
from jax.experimental import pallas as pl
from jax.experimental.pallas import tpu as pltpu
from jax.sharding import PartitionSpec as P

STEPS = 10
ROW_FIRST = (3, 4)


eps_norm = 1e-06
time_shift = 3.0
noise_level = 0.7
guidance = 4.5
loss_scale = 2048.0


def layer_norm(values):
    centred = values - jnp.mean(values, axis=-1, keepdims=True)
    inverse = lax.rsqrt(jnp.mean(centred * centred, axis=-1, keepdims=True) + eps_norm)
    return (centred * inverse, inverse)


def layer_norm_back(upstream, normed, inverse):
    return inverse * (
        upstream
        - jnp.mean(upstream, axis=-1, keepdims=True)
        - normed * jnp.mean(upstream * normed, axis=-1, keepdims=True)
    )


def rms_norm(values):
    inverse = lax.rsqrt(jnp.mean(values * values, axis=-1, keepdims=True) + eps_norm)
    return values * inverse


def plan(sample_step, step_count):
    level_now = 1.0 - sample_step.astype(jnp.float32) / step_count
    level_next = 1.0 - (sample_step + 1).astype(jnp.float32) / step_count
    time_now = time_shift * level_now / (1.0 + (time_shift - 1.0) * level_now)
    time_next = time_shift * level_next / (1.0 + (time_shift - 1.0) * level_next)
    noise_scale = noise_level * jnp.sqrt(time_now / (1.0 - time_now))
    return (time_now, time_now - time_next, noise_scale)


def transition(latent, noise_draw, velocity, sample_step, step_count):
    time_now, step_size, noise_scale = plan(sample_step, step_count)
    spread = noise_scale * jnp.sqrt(step_size)
    drift_velocity = 1.0 + noise_scale * noise_scale * (1.0 - time_now) / (2.0 * time_now)
    drift_latent = noise_scale * noise_scale / (2.0 * time_now)
    centre = latent - step_size * (drift_velocity * velocity + drift_latent * latent)
    following = centre + spread * noise_draw
    offset = following - centre
    log_density = jnp.mean(
        -offset * offset / (2.0 * spread * spread) - jnp.log(spread) - 0.5 * math.log(2.0 * math.pi)
    )
    slope = step_size * drift_velocity * offset / (spread * spread * offset.size)
    return (following, log_density, slope)


def attend_kernel(rows_ref, w_ref, text_ref, out_ref):
    passes, heads, _, pair = text_ref.shape
    width = pair // 2
    tokens = out_ref.shape[1]
    query_all, key_all, value_all = (
        jnp.dot(rows_ref[...], w_ref[k], preferred_element_type=jnp.float32) for k in range(3)
    )
    value_all = value_all.astype(jnp.bfloat16)
    score_scale = 1.0 / math.sqrt(width)
    across = (((1,), (1,)), ((), ()))
    for which in range(passes):
        here = slice(which * tokens, (which + 1) * tokens)
        outs = []
        for head in range(heads):
            lanes = slice(head * width, (head + 1) * width)
            query = rms_norm(query_all[here, lanes]).astype(jnp.bfloat16)
            key_image = rms_norm(key_all[here, lanes]).astype(jnp.bfloat16)
            text = text_ref[which, head]
            key_text = rms_norm(text[:, :width].astype(jnp.float32)).astype(jnp.bfloat16)
            image, words = (
                jnp.exp(
                    lax.dot_general(query, key, across, preferred_element_type=jnp.float32)
                    * score_scale
                )
                for key in (key_image, key_text)
            )
            total = jnp.sum(image, axis=-1, keepdims=True) + jnp.sum(words, axis=-1, keepdims=True)
            from_image = jnp.dot(
                (image / total).astype(jnp.bfloat16),
                value_all[here, lanes],
                preferred_element_type=jnp.float32,
            )
            from_text = jnp.dot(
                (words / total).astype(jnp.bfloat16), text, preferred_element_type=jnp.float32
            )
            outs.append((from_image + from_text[:, width:]).astype(jnp.bfloat16))
        out_ref[which] = jnp.concatenate(outs, 1)


def attend(stacked, w_blocks, text_pair):
    passes, _, heads, pair = text_pair.shape
    tokens = stacked.shape[0] // passes
    return pl.pallas_call(
        attend_kernel,
        out_shape=jax.ShapeDtypeStruct((passes, tokens, heads * pair // 2), jnp.bfloat16),
        in_specs=[pl.BlockSpec(memory_space=pltpu.VMEM)] * 3,
        out_specs=pl.BlockSpec(memory_space=pltpu.VMEM),
        compiler_params=pltpu.CompilerParams(vmem_limit_bytes=48 * 1024 * 1024),
    )(stacked, w_blocks, jnp.transpose(text_pair, (0, 2, 1, 3)))


def greet(peers):
    barrier = pltpu.get_barrier_semaphore()
    for there, peer in peers:
        @pl.when(there)
        def _():
            pl.semaphore_signal(
                barrier, inc=1, device_id=peer, device_id_type=pl.DeviceIdType.MESH
            )
    pl.semaphore_wait(barrier, sum(jnp.where(there, 1, 0) for there, _ in peers))


def remote(src, dst, send_sem, recv_sem, peer):
    return pltpu.make_async_remote_copy(
        src_ref=src,
        dst_ref=dst,
        send_sem=send_sem,
        recv_sem=recv_sem,
        device_id=peer,
        device_id_type=pl.DeviceIdType.MESH,
    )


def around(dp_size, line_size):
    row, spot = lax.axis_index("dp"), lax.axis_index("fsdp")
    across = [{"dp": lax.rem(row + k, dp_size)} for k in range(1, dp_size)]
    right, left = {"fsdp": lax.rem(spot + 1, line_size)}, {
        "fsdp": lax.rem(spot + line_size - 1, line_size)
    }
    has_right, has_left = spot < line_size - 1, spot > 0
    peers = [(row >= 0, peer) for peer in across] + [(has_right, right), (has_left, left)]
    return row, spot, across, (right, left), (has_right, has_left), peers


def gather_kernel(
    dp_size, line_size, row_first, blocks_ref, thin_ref, all_ref, all_thin_ref,
    local_sem, recv_sem, line_sem, across_sem,
):
    row, spot, across, sides, has_side, peers = around(dp_size, line_size)
    count = blocks_ref.shape[0]
    me = row * line_size + spot

    def mine(k):
        return blocks_ref.at[k] if k < count else thin_ref

    def slot(k, which):
        return all_ref.at[k, which] if k < count else all_thin_ref.at[which]

    def along(k, which, side, own):
        src = mine(k) if own else slot(k, which)
        return remote(
            src, slot(k, which), line_sem.at[side, k, which], recv_sem.at[k, which], sides[side]
        )

    def over(k, stop, hop, own):
        which = row * line_size + stop
        src = mine(k) if own else slot(k, which)
        return remote(
            src, slot(k, which), across_sem.at[hop, k, stop], recv_sem.at[k, which], across[hop]
        )

    def arrived(k, which):
        along(k, which, 0, False).wait_recv()

    def when(condition, action):
        @pl.when(condition)
        def _():
            action()

    order = list(range(count + 1))
    greet(peers)
    keep = [pltpu.make_async_copy(mine(k), slot(k, me), local_sem.at[k]) for k in order]
    started = []

    def go(condition, copy):
        when(condition, lambda: copy.start())
        started.append((condition, copy))

    always = row >= 0

    def own_sends(k):
        for side in (0, 1):
            go(has_side[side], along(k, me, side, True))
        for hop in range(dp_size - 1):
            go(always, over(k, spot, hop, True))

    first = [k for k in order if k in row_first]
    rest = [k for k in order if k not in row_first]
    for k in rest:
        own_sends(k)
    for copy in keep:
        copy.start()

    def pass_on(k, step, hop):
        from_row = row if hop is None else lax.rem(row + dp_size - hop - 1, dp_size)
        for side in (0, 1):
            stop = spot - step if side == 0 else spot + step
            there = stop >= 0 if side == 0 else stop < line_size
            safe = lax.rem(stop + line_size, line_size)
            which = from_row * line_size + safe
            when(there, functools.partial(arrived, k, which))
            go(there & has_side[side], along(k, which, side, False))
            if k not in row_first:
                for other in range(dp_size - 1):
                    go(there, over(k, safe, other, False))

    def row_arrivals(k):
        for hop in range(dp_size - 1):
            which = lax.rem(row + dp_size - hop - 1, dp_size) * line_size + spot
            arrived(k, which)
            if k in row_first:
                for side in (0, 1):
                    go(has_side[side], along(k, which, side, False))

    for step in range(1, line_size):
        for k in rest:
            pass_on(k, step, None)
        if step == 1:
            for k in first:
                own_sends(k)
    for k in first:
        row_arrivals(k)
    for step in range(1, line_size):
        for k in first:
            for hop in [None] + list(range(dp_size - 1)):
                pass_on(k, step, hop)
    for k in rest:
        for stop in range(line_size):
            for hop in range(dp_size - 1):
                arrived(k, lax.rem(row + dp_size - hop - 1, dp_size) * line_size + stop)
    for copy in keep:
        copy.wait()
    for condition, copy in started:
        when(condition, functools.partial(copy.wait_send))


def gather_rows(blocks, thin, dp_size, line_size):
    kinds = blocks.shape[0] + 1
    total = dp_size * line_size
    dma = pltpu.SemaphoreType.DMA
    return pl.pallas_call(
        functools.partial(gather_kernel, dp_size, line_size, ROW_FIRST),
        out_shape=(
            jax.ShapeDtypeStruct((blocks.shape[0], total) + blocks.shape[1:], blocks.dtype),
            jax.ShapeDtypeStruct((total,) + thin.shape, thin.dtype),
        ),
        in_specs=[pl.BlockSpec(memory_space=pl.ANY)] * 2,
        out_specs=(pl.BlockSpec(memory_space=pl.ANY),) * 2,
        scratch_shapes=[
            dma((kinds,)),
            dma((kinds, total)),
            dma((2, kinds, total)),
            dma((max(dp_size - 1, 1), kinds, line_size)),
        ],
        compiler_params=pltpu.CompilerParams(collective_id=0, has_side_effects=True),
    )(blocks, thin)


def scatter_kernel(
    dp_size, line_size, part_ref, out_ref, row_in, line_in, line_out,
    row_send, row_recv, line_send, line_recv,
):
    row, spot, across, sides, has_side, peers = around(dp_size, line_size)

    def over(stop, hop):
        target = lax.rem(row + hop + 1, dp_size) * line_size + stop
        return remote(
            part_ref.at[target], row_in.at[hop, stop], row_send.at[hop, stop],
            row_recv.at[hop, stop], across[hop],
        )

    def along(stop, side):
        return remote(
            line_out.at[stop], line_in.at[side, stop], line_send.at[stop],
            line_recv.at[side, stop], sides[side],
        )

    def row_sum(stop):
        value = part_ref[row * line_size + stop].astype(jnp.float32)
        for hop in range(dp_size - 1):
            over(stop, hop).wait_recv()
            value = value + row_in[hop, stop].astype(jnp.float32)
        return value

    def launch(stop):
        for hop in range(dp_size - 1):
            over(stop, hop).start()

    def step(stop, side):
        from_side = has_side[1 - side]
        line_out[stop] = row_sum(stop).astype(line_out.dtype)

        @pl.when(from_side)
        def _():
            along(stop, side).wait_recv()
            line_out[stop] = (
                line_out[stop].astype(jnp.float32) + line_in[side, stop].astype(jnp.float32)
            ).astype(line_out.dtype)

        along(stop, side).start()

    greet(peers)
    turns = []
    for turn in range(line_size - 1):
        turns.append((line_size - 1 - turn, 0))
        turns.append((turn, 1))
    for stop, side in turns:
        @pl.when(stop > spot if side == 0 else stop < spot)
        def _():
            launch(stop)
    launch(spot)
    for stop, side in turns:
        @pl.when(stop > spot if side == 0 else stop < spot)
        def _():
            step(stop, side)
    out_ref[...] = row_sum(spot)
    for side in (0, 1):
        @pl.when(has_side[1 - side])
        def _():
            along(spot, side).wait_recv()
            out_ref[...] = out_ref[...] + line_in[side, spot].astype(jnp.float32)
    for stop in range(line_size):
        for hop in range(dp_size - 1):
            over(stop, hop).wait_send()
    for stop, side in turns:
        @pl.when(stop > spot if side == 0 else stop < spot)
        def _():
            along(stop, side).wait_send()


def scatter_rows(parts, dp_size, line_size):
    block = parts.shape[1:]
    hops = max(dp_size - 1, 1)
    dma = pltpu.SemaphoreType.DMA
    return pl.pallas_call(
        functools.partial(scatter_kernel, dp_size, line_size),
        out_shape=jax.ShapeDtypeStruct(block, jnp.float32),
        in_specs=[pl.BlockSpec(memory_space=pltpu.VMEM)],
        out_specs=pl.BlockSpec(memory_space=pltpu.VMEM),
        scratch_shapes=[
            pltpu.VMEM((hops, line_size) + block, jnp.bfloat16),
            pltpu.VMEM((2, line_size) + block, jnp.bfloat16),
            pltpu.VMEM((line_size,) + block, jnp.bfloat16),
            dma((hops, line_size)),
            dma((hops, line_size)),
            dma((line_size,)),
            dma((2, line_size)),
        ],
        compiler_params=pltpu.CompilerParams(
            collective_id=1, has_side_effects=True, vmem_limit_bytes=48 * 1024 * 1024
        ),
    )(parts)


def heads_kernel(
    attended_ref, rows_ref, out_ref, total, out_first, in_first, out_second, in_second,
    send_sem, recv_sem,
):
    me = lax.axis_index("tp")
    low, high = lax.rem(me, 2), me // 2
    near, far = {"tp": me + 1 - 2 * low}, {"tp": lax.rem(me + 2, 4)}
    greet([(me >= 0, near), (me >= 0, far)])

    def product(which):
        return lax.dot_general(
            attended_ref[which], rows_ref[...], (((1,), (1,)), ((), ())),
            preferred_element_type=jnp.float32,
        )

    half = total.shape[1]
    out_first[...] = product(1 - low).astype(jnp.bfloat16)
    first = remote(out_first, in_first, send_sem.at[0], recv_sem.at[0], near)
    first.start()
    total[...] = product(low).reshape(total.shape)
    first.wait_recv()
    total[...] = total[...] + in_first[...].reshape(total.shape).astype(jnp.float32)
    out_second[...] = total[1 - high].astype(jnp.bfloat16)
    second = remote(out_second, in_second, send_sem.at[1], recv_sem.at[1], far)
    second.start()
    second.wait_recv()
    out_ref[low, high] = (total[high] + in_second[...].astype(jnp.float32)).astype(jnp.bfloat16)
    done = out_ref.at[low, high]
    third = remote(done, done, send_sem.at[2], recv_sem.at[2], far)
    third.start()
    fourth = remote(done, done, send_sem.at[3], recv_sem.at[3], near)
    fourth.start()
    remote(done, out_ref.at[low, 1 - high], send_sem.at[2], recv_sem.at[2], far).wait_recv()
    other = out_ref.at[low, 1 - high]
    fifth = remote(other, other, send_sem.at[4], recv_sem.at[4], near)
    fifth.start()
    fourth.wait_recv()
    fifth.wait_recv()
    for copy in (first, second, third, fourth, fifth):
        copy.wait_send()


def head_sum(attended, out_rows):
    _, tokens, _ = attended.shape
    width = out_rows.shape[0]
    half = tokens // 2
    return pl.pallas_call(
        heads_kernel,
        out_shape=jax.ShapeDtypeStruct((2, 2, half, width), jnp.bfloat16),
        in_specs=[pl.BlockSpec(memory_space=pltpu.VMEM)] * 2,
        out_specs=pl.BlockSpec(memory_space=pltpu.VMEM),
        scratch_shapes=[
            pltpu.VMEM((2, half, width), jnp.float32),
            pltpu.VMEM((tokens, width), jnp.bfloat16),
            pltpu.VMEM((tokens, width), jnp.bfloat16),
            pltpu.VMEM((half, width), jnp.bfloat16),
            pltpu.VMEM((half, width), jnp.bfloat16),
            pltpu.SemaphoreType.DMA((5,)),
            pltpu.SemaphoreType.DMA((5,)),
        ],
        compiler_params=pltpu.CompilerParams(
            collective_id=2, has_side_effects=True, vmem_limit_bytes=48 * 1024 * 1024
        ),
    )(attended, out_rows).reshape(2, tokens, width)


def contract_rows(left, right):
    return lax.dot_general(
        left, right, (((0,), (0,)), ((), ())), preferred_element_type=jnp.float32
    )


def local(
    hidden, text_kv, mods, latents, noise, step_index, group_id, advantages, w_qkv, w_out, w_final
):
    row_count = hidden.shape[2]
    model_width = hidden.shape[3]
    head_columns = text_kv.shape[3] * text_kv.shape[4] // 2
    residual = hidden[0].astype(jnp.float32)
    mod_values = mods[0].astype(jnp.float32)
    normed, inverse = layer_norm(residual)
    modulated = (normed * (1.0 + mod_values[:, 1:2]) + mod_values[:, 0:1]).astype(jnp.bfloat16)
    stacked = modulated.reshape(2 * row_count, model_width)
    dp_size, line_size = lax.axis_size("dp"), lax.axis_size("fsdp")
    blocks = jnp.concatenate([jnp.swapaxes(w_qkv, 0, 1), w_out[None]], 0)
    patch = w_final.shape[1]
    group_column = jnp.broadcast_to(
        group_id[:, None].astype(jnp.bfloat16), (w_final.shape[0], patch)
    )
    thin = jnp.concatenate([w_final, group_column], 1)
    gathered, all_thin = gather_rows(blocks, thin, dp_size, line_size)
    gathered = gathered.reshape(4, model_width, head_columns)
    groups = all_thin[:, 0, patch].astype(jnp.int32)
    final_rows = all_thin.reshape(model_width, -1)[:, :patch]
    out_rows = gathered[3]
    attended_flat = attend(stacked, gathered, text_kv[0])
    partial_sum = head_sum(attended_flat, out_rows).astype(jnp.float32)
    updated = residual + mod_values[:, 2:3] * partial_sum
    final_normed, final_inverse = layer_norm(updated)
    readout = (final_normed * (1.0 + mod_values[:, 4:5]) + mod_values[:, 3:4]).astype(jnp.bfloat16)
    velocity = jnp.einsum("brd,dp->brp", readout, final_rows, preferred_element_type=jnp.float32)
    guided = velocity[1] + guidance * (velocity[0] - velocity[1])
    following, log_density, slope = transition(latents[0], noise[0], guided, step_index[0], STEPS)
    members = jnp.sum((groups == group_id[0]).astype(jnp.float32))
    sample_weight = loss_scale * advantages[0] / members
    upstream_velocity = sample_weight * slope
    velocity_grad = jnp.stack(
        [guidance * upstream_velocity, (1.0 - guidance) * upstream_velocity], 0
    ).astype(jnp.bfloat16)
    readout_grad = jnp.einsum(
        "brp,dp->brd", velocity_grad, final_rows, preferred_element_type=jnp.float32
    )
    updated_grad = layer_norm_back(
        readout_grad * (1.0 + mod_values[:, 4:5]), final_normed, final_inverse
    )
    partial_grad = (mod_values[:, 2:3] * updated_grad).astype(jnp.bfloat16)
    readout_flat = readout.reshape(2 * row_count, model_width)
    velocity_flat = velocity_grad.reshape(2 * row_count, -1)
    partial_flat = partial_grad.reshape(2 * row_count, model_width)
    attended_rows = attended_flat.reshape(2 * row_count, head_columns)
    parts = jnp.concatenate(
        [
            contract_rows(partial_flat, attended_rows).astype(jnp.bfloat16),
            contract_rows(readout_flat, velocity_flat).astype(jnp.bfloat16),
        ],
        1,
    )
    sums = scatter_rows(
        parts.reshape(dp_size * line_size, -1, parts.shape[1]), dp_size, line_size
    )
    grad_out, grad_final = sums[:, :head_columns], sums[:, head_columns:]
    return (following[None], log_density[None], grad_out, grad_final)


def solution(mesh):
    in_specs = (
        P(("dp", "fsdp"), None, None, None),
        P(("dp", "fsdp"), None, None, "tp", None),
        P(("dp", "fsdp"), None, None, None),
        P(("dp", "fsdp"), None, None),
        P(("dp", "fsdp"), None, None),
        P(("dp", "fsdp")),
        P(("dp", "fsdp")),
        P(("dp", "fsdp")),
        P(("dp", "fsdp"), None, "tp"),
        P(("dp", "fsdp"), "tp"),
        P(("dp", "fsdp"), None),
    )
    out_specs = (
        P(("dp", "fsdp"), None, None),
        P(("dp", "fsdp")),
        P(("dp", "fsdp"), "tp"),
        P(("dp", "fsdp"), None),
    )
    return jax.shard_map(local, mesh=mesh, in_specs=in_specs, out_specs=out_specs, check_vma=False)
```

```python
import functools
import math

import jax
import jax.numpy as jnp
from jax import lax
from jax.experimental import pallas as pl
from jax.experimental.pallas import tpu as pltpu
from jax.sharding import PartitionSpec as P

STEPS = 10
ROW_FIRST = (4, 5)
NARROW = 128


eps_norm = 1e-06
time_shift = 3.0
noise_level = 0.7
guidance = 4.5
loss_scale = 2048.0


def layer_norm(values):
    centred = values - jnp.mean(values, axis=-1, keepdims=True)
    inverse = lax.rsqrt(jnp.mean(centred * centred, axis=-1, keepdims=True) + eps_norm)
    return (centred * inverse, inverse)


def layer_norm_back(upstream, normed, inverse):
    return inverse * (
        upstream
        - jnp.mean(upstream, axis=-1, keepdims=True)
        - normed * jnp.mean(upstream * normed, axis=-1, keepdims=True)
    )


def rms_norm(values):
    inverse = lax.rsqrt(jnp.mean(values * values, axis=-1, keepdims=True) + eps_norm)
    return values * inverse


def plan(sample_step, step_count):
    level_now = 1.0 - sample_step.astype(jnp.float32) / step_count
    level_next = 1.0 - (sample_step + 1).astype(jnp.float32) / step_count
    time_now = time_shift * level_now / (1.0 + (time_shift - 1.0) * level_now)
    time_next = time_shift * level_next / (1.0 + (time_shift - 1.0) * level_next)
    noise_scale = noise_level * jnp.sqrt(time_now / (1.0 - time_now))
    return (time_now, time_now - time_next, noise_scale)


def attend_kernel(rows_ref, w_ref, text_ref, out_ref):
    passes, heads, _, pair = text_ref.shape
    width = pair // 2
    tokens = out_ref.shape[1]
    query_all, key_all, value_all = (
        jnp.dot(rows_ref[...], w_ref[k], preferred_element_type=jnp.float32) for k in range(3)
    )
    value_all = value_all.astype(jnp.bfloat16)
    score_scale = 1.0 / math.sqrt(width)
    across = (((1,), (1,)), ((), ()))
    for which in range(passes):
        here = slice(which * tokens, (which + 1) * tokens)
        outs = []
        for head in range(heads):
            lanes = slice(head * width, (head + 1) * width)
            query = rms_norm(query_all[here, lanes]).astype(jnp.bfloat16)
            key_image = rms_norm(key_all[here, lanes]).astype(jnp.bfloat16)
            text = text_ref[which, head]
            key_text = rms_norm(text[:, :width].astype(jnp.float32)).astype(jnp.bfloat16)
            image, words = (
                jnp.exp(
                    lax.dot_general(query, key, across, preferred_element_type=jnp.float32)
                    * score_scale
                )
                for key in (key_image, key_text)
            )
            total = jnp.sum(image, axis=-1, keepdims=True) + jnp.sum(words, axis=-1, keepdims=True)
            from_image = jnp.dot(
                (image / total).astype(jnp.bfloat16),
                value_all[here, lanes],
                preferred_element_type=jnp.float32,
            )
            from_text = jnp.dot(
                (words / total).astype(jnp.bfloat16), text, preferred_element_type=jnp.float32
            )
            outs.append((from_image + from_text[:, width:]).astype(jnp.bfloat16))
        out_ref[which] = jnp.concatenate(outs, 1)


def attend(stacked, w_blocks, text_pair):
    passes, _, heads, pair = text_pair.shape
    tokens = stacked.shape[0] // passes
    return pl.pallas_call(
        attend_kernel,
        out_shape=jax.ShapeDtypeStruct((passes, tokens, heads * pair // 2), jnp.bfloat16),
        in_specs=[pl.BlockSpec(memory_space=pltpu.VMEM)] * 3,
        out_specs=pl.BlockSpec(memory_space=pltpu.VMEM),
        compiler_params=pltpu.CompilerParams(vmem_limit_bytes=48 * 1024 * 1024),
    )(stacked, w_blocks, jnp.transpose(text_pair, (0, 2, 1, 3)))


def greet(peers):
    barrier = pltpu.get_barrier_semaphore()
    for there, peer in peers:
        @pl.when(there)
        def _():
            pl.semaphore_signal(
                barrier, inc=1, device_id=peer, device_id_type=pl.DeviceIdType.MESH
            )
    pl.semaphore_wait(barrier, sum(jnp.where(there, 1, 0) for there, _ in peers))


def remote(src, dst, send_sem, recv_sem, peer):
    return pltpu.make_async_remote_copy(
        src_ref=src,
        dst_ref=dst,
        send_sem=send_sem,
        recv_sem=recv_sem,
        device_id=peer,
        device_id_type=pl.DeviceIdType.MESH,
    )


def around(dp_size, line_size):
    row, spot = lax.axis_index("dp"), lax.axis_index("fsdp")
    across = [{"dp": lax.rem(row + k, dp_size)} for k in range(1, dp_size)]
    right, left = {"fsdp": lax.rem(spot + 1, line_size)}, {
        "fsdp": lax.rem(spot + line_size - 1, line_size)
    }
    has_right, has_left = spot < line_size - 1, spot > 0
    peers = [(row >= 0, peer) for peer in across] + [(has_right, right), (has_left, left)]
    return row, spot, across, (right, left), (has_right, has_left), peers


def gather_kernel(
    dp_size, line_size, row_first, blocks_ref, thin_ref, all_ref, all_thin_ref,
    local_sem, recv_sem, line_sem, across_sem,
):
    row, spot, across, sides, has_side, peers = around(dp_size, line_size)
    count = blocks_ref.shape[0]
    cut = blocks_ref.shape[2] - NARROW
    me = row * line_size + spot

    def mine(k):
        if k > count:
            return thin_ref
        if k == count:
            return blocks_ref.at[count - 1, :, pl.ds(cut, NARROW)]
        return blocks_ref.at[k, :, pl.ds(0, cut)] if k == count - 1 else blocks_ref.at[k]

    def slot(k, which):
        if k > count:
            return all_thin_ref.at[which]
        if k == count:
            return all_ref.at[count - 1, which, :, pl.ds(cut, NARROW)]
        return all_ref.at[k, which, :, pl.ds(0, cut)] if k == count - 1 else all_ref.at[k, which]

    def along(k, which, side, own):
        src = mine(k) if own else slot(k, which)
        return remote(
            src, slot(k, which), line_sem.at[side, k, which], recv_sem.at[k, which], sides[side]
        )

    def over(k, stop, hop, own):
        which = row * line_size + stop
        src = mine(k) if own else slot(k, which)
        return remote(
            src, slot(k, which), across_sem.at[hop, k, stop], recv_sem.at[k, which], across[hop]
        )

    def arrived(k, which):
        along(k, which, 0, False).wait_recv()

    def when(condition, action):
        @pl.when(condition)
        def _():
            action()

    order = list(range(count + 2))
    greet(peers)
    keep = [pltpu.make_async_copy(mine(k), slot(k, me), local_sem.at[k]) for k in order]
    started = []

    def go(condition, copy):
        when(condition, lambda: copy.start())
        started.append((condition, copy))

    always = row >= 0

    def own_sends(k):
        for side in (0, 1):
            go(has_side[side], along(k, me, side, True))
        for hop in range(dp_size - 1):
            go(always, over(k, spot, hop, True))

    first = [k for k in order if k in row_first]
    rest = [k for k in order if k not in row_first]
    for k in rest:
        own_sends(k)
    for copy in keep:
        copy.start()

    def pass_on(k, step, hop):
        from_row = row if hop is None else lax.rem(row + dp_size - hop - 1, dp_size)
        for side in (0, 1):
            stop = spot - step if side == 0 else spot + step
            there = stop >= 0 if side == 0 else stop < line_size
            safe = lax.rem(stop + line_size, line_size)
            which = from_row * line_size + safe
            when(there, functools.partial(arrived, k, which))
            go(there & has_side[side], along(k, which, side, False))
            if k not in row_first:
                for other in range(dp_size - 1):
                    go(there, over(k, safe, other, False))

    def row_arrivals(k):
        for hop in range(dp_size - 1):
            which = lax.rem(row + dp_size - hop - 1, dp_size) * line_size + spot
            arrived(k, which)
            if k in row_first:
                for side in (0, 1):
                    go(has_side[side], along(k, which, side, False))

    for step in range(1, line_size):
        for k in rest:
            pass_on(k, step, None)
        if step == 1:
            for k in first:
                own_sends(k)
    for k in first:
        row_arrivals(k)
    for step in range(1, line_size):
        for k in first:
            for hop in [None] + list(range(dp_size - 1)):
                pass_on(k, step, hop)
    for k in rest:
        for stop in range(line_size):
            for hop in range(dp_size - 1):
                arrived(k, lax.rem(row + dp_size - hop - 1, dp_size) * line_size + stop)
    for copy in keep:
        copy.wait()
    for condition, copy in started:
        when(condition, functools.partial(copy.wait_send))


def gather_rows(blocks, thin, dp_size, line_size):
    kinds = blocks.shape[0] + 2
    total = dp_size * line_size
    dma = pltpu.SemaphoreType.DMA
    return pl.pallas_call(
        functools.partial(gather_kernel, dp_size, line_size, ROW_FIRST),
        out_shape=(
            jax.ShapeDtypeStruct((blocks.shape[0], total) + blocks.shape[1:], blocks.dtype),
            jax.ShapeDtypeStruct((total,) + thin.shape, thin.dtype),
        ),
        in_specs=[pl.BlockSpec(memory_space=pl.ANY)] * 2,
        out_specs=(pl.BlockSpec(memory_space=pl.ANY),) * 2,
        scratch_shapes=[
            dma((kinds,)),
            dma((kinds, total)),
            dma((2, kinds, total)),
            dma((max(dp_size - 1, 1), kinds, line_size)),
        ],
        compiler_params=pltpu.CompilerParams(collective_id=0, has_side_effects=True),
    )(blocks, thin)


def scatter_kernel(
    dp_size, line_size, part_ref, out_ref, row_in, line_in, line_out,
    row_send, row_recv, line_send, line_recv,
):
    row, spot, across, sides, has_side, peers = around(dp_size, line_size)

    def over(stop, hop):
        target = lax.rem(row + hop + 1, dp_size) * line_size + stop
        return remote(
            part_ref.at[target], row_in.at[hop, stop], row_send.at[hop, stop],
            row_recv.at[hop, stop], across[hop],
        )

    def along(stop, side):
        return remote(
            line_out.at[stop], line_in.at[side, stop], line_send.at[stop],
            line_recv.at[side, stop], sides[side],
        )

    def row_sum(stop):
        value = part_ref[row * line_size + stop].astype(jnp.float32)
        for hop in range(dp_size - 1):
            over(stop, hop).wait_recv()
            value = value + row_in[hop, stop].astype(jnp.float32)
        return value

    def launch(stop):
        for hop in range(dp_size - 1):
            over(stop, hop).start()

    def step(stop, side):
        from_side = has_side[1 - side]
        line_out[stop] = row_sum(stop).astype(line_out.dtype)

        @pl.when(from_side)
        def _():
            along(stop, side).wait_recv()
            line_out[stop] = (
                line_out[stop].astype(jnp.float32) + line_in[side, stop].astype(jnp.float32)
            ).astype(line_out.dtype)

        along(stop, side).start()

    greet(peers)
    turns = []
    for turn in range(line_size - 1):
        turns.append((line_size - 1 - turn, 0))
        turns.append((turn, 1))
    for stop, side in turns:
        @pl.when(stop > spot if side == 0 else stop < spot)
        def _():
            launch(stop)
    launch(spot)
    for stop, side in turns:
        @pl.when(stop > spot if side == 0 else stop < spot)
        def _():
            step(stop, side)
    out_ref[...] = row_sum(spot)
    for side in (0, 1):
        @pl.when(has_side[1 - side])
        def _():
            along(spot, side).wait_recv()
            out_ref[...] = out_ref[...] + line_in[side, spot].astype(jnp.float32)
    for stop in range(line_size):
        for hop in range(dp_size - 1):
            over(stop, hop).wait_send()
    for stop, side in turns:
        @pl.when(stop > spot if side == 0 else stop < spot)
        def _():
            along(stop, side).wait_send()


def scatter_rows(parts, dp_size, line_size):
    block = parts.shape[1:]
    hops = max(dp_size - 1, 1)
    dma = pltpu.SemaphoreType.DMA
    return pl.pallas_call(
        functools.partial(scatter_kernel, dp_size, line_size),
        out_shape=jax.ShapeDtypeStruct(block, jnp.float32),
        in_specs=[pl.BlockSpec(memory_space=pltpu.VMEM)],
        out_specs=pl.BlockSpec(memory_space=pltpu.VMEM),
        scratch_shapes=[
            pltpu.VMEM((hops, line_size) + block, jnp.bfloat16),
            pltpu.VMEM((2, line_size) + block, jnp.bfloat16),
            pltpu.VMEM((line_size,) + block, jnp.bfloat16),
            dma((hops, line_size)),
            dma((hops, line_size)),
            dma((line_size,)),
            dma((2, line_size)),
        ],
        compiler_params=pltpu.CompilerParams(
            collective_id=1, has_side_effects=True, vmem_limit_bytes=48 * 1024 * 1024
        ),
    )(parts)


def heads_kernel(
    attended_ref, rows_ref, out_ref, total, out_first, in_first, out_second, in_second,
    send_sem, recv_sem,
):
    me = lax.axis_index("tp")
    low, high = lax.rem(me, 2), me // 2
    near, far = {"tp": me + 1 - 2 * low}, {"tp": lax.rem(me + 2, 4)}
    greet([(me >= 0, near), (me >= 0, far)])

    def product(which):
        return lax.dot_general(
            attended_ref[which], rows_ref[...], (((1,), (1,)), ((), ())),
            preferred_element_type=jnp.float32,
        )

    half = total.shape[1]
    out_first[...] = product(1 - low).astype(jnp.bfloat16)
    first = remote(out_first, in_first, send_sem.at[0], recv_sem.at[0], near)
    first.start()
    total[...] = product(low).reshape(total.shape)
    first.wait_recv()
    total[...] = total[...] + in_first[...].reshape(total.shape).astype(jnp.float32)
    out_second[...] = total[1 - high].astype(jnp.bfloat16)
    second = remote(out_second, in_second, send_sem.at[1], recv_sem.at[1], far)
    second.start()
    second.wait_recv()
    out_ref[low, high] = (total[high] + in_second[...].astype(jnp.float32)).astype(jnp.bfloat16)
    done = out_ref.at[low, high]
    third = remote(done, done, send_sem.at[2], recv_sem.at[2], far)
    third.start()
    fourth = remote(done, done, send_sem.at[3], recv_sem.at[3], near)
    fourth.start()
    remote(done, out_ref.at[low, 1 - high], send_sem.at[2], recv_sem.at[2], far).wait_recv()
    other = out_ref.at[low, 1 - high]
    fifth = remote(other, other, send_sem.at[4], recv_sem.at[4], near)
    fifth.start()
    fourth.wait_recv()
    fifth.wait_recv()
    for copy in (first, second, third, fourth, fifth):
        copy.wait_send()


def head_sum(attended, out_rows):
    _, tokens, _ = attended.shape
    width = out_rows.shape[0]
    half = tokens // 2
    return pl.pallas_call(
        heads_kernel,
        out_shape=jax.ShapeDtypeStruct((2, 2, half, width), jnp.bfloat16),
        in_specs=[pl.BlockSpec(memory_space=pltpu.VMEM)] * 2,
        out_specs=pl.BlockSpec(memory_space=pltpu.VMEM),
        scratch_shapes=[
            pltpu.VMEM((2, half, width), jnp.float32),
            pltpu.VMEM((tokens, width), jnp.bfloat16),
            pltpu.VMEM((tokens, width), jnp.bfloat16),
            pltpu.VMEM((half, width), jnp.bfloat16),
            pltpu.VMEM((half, width), jnp.bfloat16),
            pltpu.SemaphoreType.DMA((5,)),
            pltpu.SemaphoreType.DMA((5,)),
        ],
        compiler_params=pltpu.CompilerParams(
            collective_id=2, has_side_effects=True, vmem_limit_bytes=48 * 1024 * 1024
        ),
    )(attended, out_rows).reshape(2, tokens, width)


def contract_rows(left, right):
    return lax.dot_general(
        left, right, (((0,), (0,)), ((), ())), preferred_element_type=jnp.float32
    )


def middle_kernel(
    scalar_ref, hidden_ref, sum_ref, mods_ref, final_ref, latent_ref, noise_ref, attended_ref,
    next_ref, offset_ref, parts_ref, normed_ref, readout_ref, grad_ref,
):
    spread, step_size, drift_velocity, drift_latent, sample_weight = (
        scalar_ref[k] for k in range(5)
    )
    passes, tokens, _ = hidden_ref.shape
    inverses, velocity = [], []
    for which in range(passes):
        updated = hidden_ref[which].astype(jnp.float32) + mods_ref[which, 2:3] * sum_ref[
            which
        ].astype(jnp.float32)
        normed, inverse = layer_norm(updated)
        normed_ref[which] = normed
        inverses.append(inverse)
        readout = (normed * (1.0 + mods_ref[which, 4:5]) + mods_ref[which, 3:4]).astype(
            jnp.bfloat16
        )
        readout_ref[which * tokens : (which + 1) * tokens] = readout
        velocity.append(jnp.dot(readout, final_ref[...], preferred_element_type=jnp.float32))
    guided = velocity[1] + guidance * (velocity[0] - velocity[1])
    latent = latent_ref[...]
    centre = latent - step_size * (drift_velocity * guided + drift_latent * latent)
    following = centre + spread * noise_ref[...]
    offset = following - centre
    next_ref[...] = following
    offset_ref[...] = offset
    slope = step_size * drift_velocity * offset / (spread * spread * offset.size)
    upstream = sample_weight * slope
    grads = [
        (factor * upstream).astype(jnp.bfloat16) for factor in (guidance, 1.0 - guidance)
    ]
    for which in range(passes):
        readout_grad = lax.dot_general(
            grads[which], final_ref[...], (((1,), (1,)), ((), ())),
            preferred_element_type=jnp.float32,
        )
        updated_grad = layer_norm_back(
            readout_grad * (1.0 + mods_ref[which, 4:5]), normed_ref[which], inverses[which]
        )
        grad_ref[which * tokens : (which + 1) * tokens] = (
            mods_ref[which, 2:3] * updated_grad
        ).astype(jnp.bfloat16)
    columns = attended_ref.shape[1]
    parts_ref[:, :columns] = contract_rows(grad_ref[...], attended_ref[...]).astype(jnp.bfloat16)
    parts_ref[:, columns:] = contract_rows(
        readout_ref[...], jnp.concatenate(grads, 0)
    ).astype(jnp.bfloat16)


def middle(scalars, hidden, total, mods, final_rows, latent, noise, attended):
    passes, tokens, model_width = hidden.shape
    whole = pl.BlockSpec(memory_space=pltpu.VMEM)
    return pl.pallas_call(
        middle_kernel,
        out_shape=(
            jax.ShapeDtypeStruct(latent.shape, jnp.float32),
            jax.ShapeDtypeStruct(latent.shape, jnp.float32),
            jax.ShapeDtypeStruct(
                (model_width, attended.shape[1] + final_rows.shape[1]), jnp.bfloat16
            ),
        ),
        in_specs=[pl.BlockSpec(memory_space=pltpu.SMEM)] + [whole] * 7,
        out_specs=(whole,) * 3,
        scratch_shapes=[
            pltpu.VMEM((passes, tokens, model_width), jnp.float32),
            pltpu.VMEM((passes * tokens, model_width), jnp.bfloat16),
            pltpu.VMEM((passes * tokens, model_width), jnp.bfloat16),
        ],
        compiler_params=pltpu.CompilerParams(vmem_limit_bytes=48 * 1024 * 1024),
    )(scalars, hidden, total, mods, final_rows, latent, noise, attended)


def local(
    hidden, text_kv, mods, latents, noise, step_index, group_id, advantages, w_qkv, w_out, w_final
):
    row_count = hidden.shape[2]
    model_width = hidden.shape[3]
    head_columns = text_kv.shape[3] * text_kv.shape[4] // 2
    residual = hidden[0].astype(jnp.float32)
    mod_values = mods[0].astype(jnp.float32)
    normed, inverse = layer_norm(residual)
    modulated = (normed * (1.0 + mod_values[:, 1:2]) + mod_values[:, 0:1]).astype(jnp.bfloat16)
    stacked = modulated.reshape(2 * row_count, model_width)
    dp_size, line_size = lax.axis_size("dp"), lax.axis_size("fsdp")
    blocks = jnp.concatenate([jnp.swapaxes(w_qkv, 0, 1), w_out[None]], 0)
    patch = w_final.shape[1]
    group_column = jnp.broadcast_to(
        group_id[:, None].astype(jnp.bfloat16), (w_final.shape[0], patch)
    )
    thin = jnp.concatenate([w_final, group_column], 1)
    gathered, all_thin = gather_rows(blocks, thin, dp_size, line_size)
    gathered = gathered.reshape(4, model_width, head_columns)
    groups = all_thin[:, 0, patch].astype(jnp.int32)
    final_rows = all_thin.reshape(model_width, -1)[:, :patch]
    out_rows = gathered[3]
    attended_flat = attend(stacked, gathered, text_kv[0])
    total = head_sum(attended_flat, out_rows)
    time_now, step_size, noise_scale = plan(step_index[0], STEPS)
    spread = noise_scale * jnp.sqrt(step_size)
    drift_velocity = 1.0 + noise_scale * noise_scale * (1.0 - time_now) / (2.0 * time_now)
    drift_latent = noise_scale * noise_scale / (2.0 * time_now)
    members = jnp.sum((groups == group_id[0]).astype(jnp.float32))
    sample_weight = loss_scale * advantages[0] / members
    scalars = jnp.stack([spread, step_size, drift_velocity, drift_latent, sample_weight])
    following, offset, parts = middle(
        scalars, hidden[0], total, mod_values, final_rows, latents[0], noise[0],
        attended_flat.reshape(2 * row_count, head_columns),
    )
    log_density = jnp.mean(
        -offset * offset / (2.0 * spread * spread)
        - jnp.log(spread)
        - 0.5 * math.log(2.0 * math.pi)
    )
    sums = scatter_rows(
        parts.reshape(dp_size * line_size, -1, parts.shape[1]), dp_size, line_size
    )
    grad_out, grad_final = sums[:, :head_columns], sums[:, head_columns:]
    return (following[None], log_density[None], grad_out, grad_final)


def solution(mesh):
    in_specs = (
        P(("dp", "fsdp"), None, None, None),
        P(("dp", "fsdp"), None, None, "tp", None),
        P(("dp", "fsdp"), None, None, None),
        P(("dp", "fsdp"), None, None),
        P(("dp", "fsdp"), None, None),
        P(("dp", "fsdp")),
        P(("dp", "fsdp")),
        P(("dp", "fsdp")),
        P(("dp", "fsdp"), None, "tp"),
        P(("dp", "fsdp"), "tp"),
        P(("dp", "fsdp"), None),
    )
    out_specs = (
        P(("dp", "fsdp"), None, None),
        P(("dp", "fsdp")),
        P(("dp", "fsdp"), "tp"),
        P(("dp", "fsdp"), None),
    )
    return jax.shard_map(local, mesh=mesh, in_specs=in_specs, out_specs=out_specs, check_vma=False)
```

```python
import functools
import math

import jax
import jax.numpy as jnp
from jax import lax
from jax.experimental import pallas as pl
from jax.experimental.pallas import tpu as pltpu
from jax.sharding import PartitionSpec as P

STEPS = 10
ROW_FIRST = (4, 5)
NARROW = 128


eps_norm = 1e-06
time_shift = 3.0
noise_level = 0.7
guidance = 4.5
loss_scale = 2048.0


def layer_norm(values):
    centred = values - jnp.mean(values, axis=-1, keepdims=True)
    inverse = lax.rsqrt(jnp.mean(centred * centred, axis=-1, keepdims=True) + eps_norm)
    return (centred * inverse, inverse)


def layer_norm_back(upstream, normed, inverse):
    return inverse * (
        upstream
        - jnp.mean(upstream, axis=-1, keepdims=True)
        - normed * jnp.mean(upstream * normed, axis=-1, keepdims=True)
    )


def rms_norm(values):
    inverse = lax.rsqrt(jnp.mean(values * values, axis=-1, keepdims=True) + eps_norm)
    return values * inverse


def plan(sample_step, step_count):
    level_now = 1.0 - sample_step.astype(jnp.float32) / step_count
    level_next = 1.0 - (sample_step + 1).astype(jnp.float32) / step_count
    time_now = time_shift * level_now / (1.0 + (time_shift - 1.0) * level_now)
    time_next = time_shift * level_next / (1.0 + (time_shift - 1.0) * level_next)
    noise_scale = noise_level * jnp.sqrt(time_now / (1.0 - time_now))
    return (time_now, time_now - time_next, noise_scale)


def attend_kernel(rows_ref, w_ref, text_ref, out_ref):
    passes, heads, _, pair = text_ref.shape
    width = pair // 2
    tokens = out_ref.shape[1]
    query_all, key_all, value_all = (
        jnp.dot(rows_ref[...], w_ref[k], preferred_element_type=jnp.float32) for k in range(3)
    )
    value_all = value_all.astype(jnp.bfloat16)
    score_scale = 1.0 / math.sqrt(width)
    across = (((1,), (1,)), ((), ()))
    for which in range(passes):
        here = slice(which * tokens, (which + 1) * tokens)
        outs = []
        for head in range(heads):
            lanes = slice(head * width, (head + 1) * width)
            query = rms_norm(query_all[here, lanes]).astype(jnp.bfloat16)
            key_image = rms_norm(key_all[here, lanes]).astype(jnp.bfloat16)
            text = text_ref[which, head]
            key_text = rms_norm(text[:, :width].astype(jnp.float32)).astype(jnp.bfloat16)
            image, words = (
                jnp.exp(
                    lax.dot_general(query, key, across, preferred_element_type=jnp.float32)
                    * score_scale
                )
                for key in (key_image, key_text)
            )
            total = jnp.sum(image, axis=-1, keepdims=True) + jnp.sum(words, axis=-1, keepdims=True)
            from_image = jnp.dot(
                (image / total).astype(jnp.bfloat16),
                value_all[here, lanes],
                preferred_element_type=jnp.float32,
            )
            from_text = jnp.dot(
                (words / total).astype(jnp.bfloat16), text, preferred_element_type=jnp.float32
            )
            outs.append((from_image + from_text[:, width:]).astype(jnp.bfloat16))
        out_ref[which] = jnp.concatenate(outs, 1)


def attend(stacked, w_blocks, text_pair):
    passes, _, heads, pair = text_pair.shape
    tokens = stacked.shape[0] // passes
    return pl.pallas_call(
        attend_kernel,
        out_shape=jax.ShapeDtypeStruct((passes, tokens, heads * pair // 2), jnp.bfloat16),
        in_specs=[pl.BlockSpec(memory_space=pltpu.VMEM)] * 3,
        out_specs=pl.BlockSpec(memory_space=pltpu.VMEM),
        compiler_params=pltpu.CompilerParams(vmem_limit_bytes=48 * 1024 * 1024),
    )(stacked, w_blocks, jnp.transpose(text_pair, (0, 2, 1, 3)))


def greet(peers):
    barrier = pltpu.get_barrier_semaphore()
    for there, peer in peers:
        @pl.when(there)
        def _():
            pl.semaphore_signal(
                barrier, inc=1, device_id=peer, device_id_type=pl.DeviceIdType.MESH
            )
    pl.semaphore_wait(barrier, sum(jnp.where(there, 1, 0) for there, _ in peers))


def remote(src, dst, send_sem, recv_sem, peer):
    return pltpu.make_async_remote_copy(
        src_ref=src,
        dst_ref=dst,
        send_sem=send_sem,
        recv_sem=recv_sem,
        device_id=peer,
        device_id_type=pl.DeviceIdType.MESH,
    )


def around(dp_size, line_size):
    row, spot = lax.axis_index("dp"), lax.axis_index("fsdp")
    across = [{"dp": lax.rem(row + k, dp_size)} for k in range(1, dp_size)]
    right, left = {"fsdp": lax.rem(spot + 1, line_size)}, {
        "fsdp": lax.rem(spot + line_size - 1, line_size)
    }
    has_right, has_left = spot < line_size - 1, spot > 0
    peers = [(row >= 0, peer) for peer in across] + [(has_right, right), (has_left, left)]
    return row, spot, across, (right, left), (has_right, has_left), peers


def gather_kernel(
    dp_size, line_size, row_first, blocks_ref, last_ref, thin_ref, all_ref, all_last_ref,
    all_thin_ref,
    local_sem, recv_sem, line_sem, across_sem,
):
    row, spot, across, sides, has_side, peers = around(dp_size, line_size)
    count = blocks_ref.shape[0] + 1
    cut = last_ref.shape[1] - NARROW
    me = row * line_size + spot

    def mine(k):
        if k > count:
            return thin_ref
        if k == count:
            return last_ref.at[:, pl.ds(cut, NARROW)]
        return last_ref.at[:, pl.ds(0, cut)] if k == count - 1 else blocks_ref.at[k]

    def slot(k, which):
        if k > count:
            return all_thin_ref.at[which]
        if k == count:
            return all_last_ref.at[which, :, pl.ds(cut, NARROW)]
        return all_last_ref.at[which, :, pl.ds(0, cut)] if k == count - 1 else all_ref.at[k, which]

    def along(k, which, side, own):
        src = mine(k) if own else slot(k, which)
        return remote(
            src, slot(k, which), line_sem.at[side, k, which], recv_sem.at[k, which], sides[side]
        )

    def over(k, stop, hop, own):
        which = row * line_size + stop
        src = mine(k) if own else slot(k, which)
        return remote(
            src, slot(k, which), across_sem.at[hop, k, stop], recv_sem.at[k, which], across[hop]
        )

    def arrived(k, which):
        along(k, which, 0, False).wait_recv()

    def when(condition, action):
        @pl.when(condition)
        def _():
            action()

    order = list(range(count + 2))
    greet(peers)
    keep = [pltpu.make_async_copy(mine(k), slot(k, me), local_sem.at[k]) for k in order]
    started = []

    def go(condition, copy):
        when(condition, lambda: copy.start())
        started.append((condition, copy))

    always = row >= 0

    def own_sends(k):
        for side in (0, 1):
            go(has_side[side], along(k, me, side, True))
        for hop in range(dp_size - 1):
            go(always, over(k, spot, hop, True))

    first = [k for k in order if k in row_first]
    rest = [k for k in order if k not in row_first]
    for k in rest:
        own_sends(k)
    for copy in keep:
        copy.start()

    def pass_on(k, step, hop):
        from_row = row if hop is None else lax.rem(row + dp_size - hop - 1, dp_size)
        for side in (0, 1):
            stop = spot - step if side == 0 else spot + step
            there = stop >= 0 if side == 0 else stop < line_size
            safe = lax.rem(stop + line_size, line_size)
            which = from_row * line_size + safe
            when(there, functools.partial(arrived, k, which))
            go(there & has_side[side], along(k, which, side, False))
            if k not in row_first:
                for other in range(dp_size - 1):
                    go(there, over(k, safe, other, False))

    def row_arrivals(k):
        for hop in range(dp_size - 1):
            which = lax.rem(row + dp_size - hop - 1, dp_size) * line_size + spot
            arrived(k, which)
            if k in row_first:
                for side in (0, 1):
                    go(has_side[side], along(k, which, side, False))

    for step in range(1, line_size):
        for k in rest:
            pass_on(k, step, None)
        if step == 1:
            for k in first:
                own_sends(k)
    for k in first:
        row_arrivals(k)
    for step in range(1, line_size):
        for k in first:
            for hop in [None] + list(range(dp_size - 1)):
                pass_on(k, step, hop)
    for k in rest:
        for stop in range(line_size):
            for hop in range(dp_size - 1):
                arrived(k, lax.rem(row + dp_size - hop - 1, dp_size) * line_size + stop)
    for copy in keep:
        copy.wait()
    for condition, copy in started:
        when(condition, functools.partial(copy.wait_send))


def gather_rows(blocks, last, thin, dp_size, line_size):
    kinds = blocks.shape[0] + 3
    total = dp_size * line_size
    dma = pltpu.SemaphoreType.DMA
    return pl.pallas_call(
        functools.partial(gather_kernel, dp_size, line_size, ROW_FIRST),
        out_shape=(
            jax.ShapeDtypeStruct((blocks.shape[0], total) + blocks.shape[1:], blocks.dtype),
            jax.ShapeDtypeStruct((total,) + last.shape, last.dtype),
            jax.ShapeDtypeStruct((total,) + thin.shape, thin.dtype),
        ),
        in_specs=[pl.BlockSpec(memory_space=pl.ANY)] * 3,
        out_specs=(pl.BlockSpec(memory_space=pl.ANY),) * 3,
        scratch_shapes=[
            dma((kinds,)),
            dma((kinds, total)),
            dma((2, kinds, total)),
            dma((max(dp_size - 1, 1), kinds, line_size)),
        ],
        compiler_params=pltpu.CompilerParams(collective_id=0, has_side_effects=True),
    )(blocks, last, thin)


def scatter_kernel(
    dp_size, line_size, part_ref, wide_ref, thin_ref, row_in, line_in, line_out,
    row_send, row_recv, line_send, line_recv,
):
    row, spot, across, sides, has_side, peers = around(dp_size, line_size)

    def over(stop, hop):
        target = lax.rem(row + hop + 1, dp_size) * line_size + stop
        return remote(
            part_ref.at[target], row_in.at[hop, stop], row_send.at[hop, stop],
            row_recv.at[hop, stop], across[hop],
        )

    def along(stop, side):
        return remote(
            line_out.at[stop], line_in.at[side, stop], line_send.at[stop],
            line_recv.at[side, stop], sides[side],
        )

    def row_sum(stop):
        value = part_ref[row * line_size + stop].astype(jnp.float32)
        for hop in range(dp_size - 1):
            over(stop, hop).wait_recv()
            value = value + row_in[hop, stop].astype(jnp.float32)
        return value

    def launch(stop):
        for hop in range(dp_size - 1):
            over(stop, hop).start()

    def step(stop, side):
        from_side = has_side[1 - side]
        line_out[stop] = row_sum(stop).astype(line_out.dtype)

        @pl.when(from_side)
        def _():
            along(stop, side).wait_recv()
            line_out[stop] = (
                line_out[stop].astype(jnp.float32) + line_in[side, stop].astype(jnp.float32)
            ).astype(line_out.dtype)

        along(stop, side).start()

    greet(peers)
    turns = []
    for turn in range(line_size - 1):
        turns.append((line_size - 1 - turn, 0))
        turns.append((turn, 1))
    for stop, side in turns:
        @pl.when(stop > spot if side == 0 else stop < spot)
        def _():
            launch(stop)
    launch(spot)
    for stop, side in turns:
        @pl.when(stop > spot if side == 0 else stop < spot)
        def _():
            step(stop, side)
    value = row_sum(spot)
    columns = wide_ref.shape[1]
    wide_ref[...] = value[:, :columns]
    thin_ref[...] = value[:, columns:]
    for side in (0, 1):
        @pl.when(has_side[1 - side])
        def _():
            along(spot, side).wait_recv()
            extra = line_in[side, spot].astype(jnp.float32)
            wide_ref[...] = wide_ref[...] + extra[:, :columns]
            thin_ref[...] = thin_ref[...] + extra[:, columns:]
    for stop in range(line_size):
        for hop in range(dp_size - 1):
            over(stop, hop).wait_send()
    for stop, side in turns:
        @pl.when(stop > spot if side == 0 else stop < spot)
        def _():
            along(stop, side).wait_send()


def scatter_rows(parts, columns, dp_size, line_size):
    block = parts.shape[1:]
    hops = max(dp_size - 1, 1)
    dma = pltpu.SemaphoreType.DMA
    return pl.pallas_call(
        functools.partial(scatter_kernel, dp_size, line_size),
        out_shape=(
            jax.ShapeDtypeStruct((block[0], columns), jnp.float32),
            jax.ShapeDtypeStruct((block[0], block[1] - columns), jnp.float32),
        ),
        in_specs=[pl.BlockSpec(memory_space=pltpu.VMEM)],
        out_specs=(pl.BlockSpec(memory_space=pltpu.VMEM),) * 2,
        scratch_shapes=[
            pltpu.VMEM((hops, line_size) + block, jnp.bfloat16),
            pltpu.VMEM((2, line_size) + block, jnp.bfloat16),
            pltpu.VMEM((line_size,) + block, jnp.bfloat16),
            dma((hops, line_size)),
            dma((hops, line_size)),
            dma((line_size,)),
            dma((2, line_size)),
        ],
        compiler_params=pltpu.CompilerParams(
            collective_id=1, has_side_effects=True, vmem_limit_bytes=48 * 1024 * 1024
        ),
    )(parts)


def heads_kernel(
    attended_ref, rows_ref, out_ref, total, out_first, in_first, out_second, in_second,
    send_sem, recv_sem,
):
    me = lax.axis_index("tp")
    low, high = lax.rem(me, 2), me // 2
    near, far = {"tp": me + 1 - 2 * low}, {"tp": lax.rem(me + 2, 4)}
    greet([(me >= 0, near), (me >= 0, far)])

    def product(which):
        return lax.dot_general(
            attended_ref[which], rows_ref[...], (((1,), (1,)), ((), ())),
            preferred_element_type=jnp.float32,
        )

    half = total.shape[1]
    out_first[...] = product(1 - low).astype(jnp.bfloat16)
    first = remote(out_first, in_first, send_sem.at[0], recv_sem.at[0], near)
    first.start()
    total[...] = product(low).reshape(total.shape)
    first.wait_recv()
    total[...] = total[...] + in_first[...].reshape(total.shape).astype(jnp.float32)
    out_second[...] = total[1 - high].astype(jnp.bfloat16)
    second = remote(out_second, in_second, send_sem.at[1], recv_sem.at[1], far)
    second.start()
    second.wait_recv()
    out_ref[low, high] = (total[high] + in_second[...].astype(jnp.float32)).astype(jnp.bfloat16)
    done = out_ref.at[low, high]
    third = remote(done, done, send_sem.at[2], recv_sem.at[2], far)
    third.start()
    fourth = remote(done, done, send_sem.at[3], recv_sem.at[3], near)
    fourth.start()
    remote(done, out_ref.at[low, 1 - high], send_sem.at[2], recv_sem.at[2], far).wait_recv()
    other = out_ref.at[low, 1 - high]
    fifth = remote(other, other, send_sem.at[4], recv_sem.at[4], near)
    fifth.start()
    fourth.wait_recv()
    fifth.wait_recv()
    for copy in (first, second, third, fourth, fifth):
        copy.wait_send()


def head_sum(attended, out_rows):
    _, tokens, _ = attended.shape
    width = out_rows.shape[0]
    half = tokens // 2
    return pl.pallas_call(
        heads_kernel,
        out_shape=jax.ShapeDtypeStruct((2, 2, half, width), jnp.bfloat16),
        in_specs=[pl.BlockSpec(memory_space=pltpu.VMEM)] * 2,
        out_specs=pl.BlockSpec(memory_space=pltpu.VMEM),
        scratch_shapes=[
            pltpu.VMEM((2, half, width), jnp.float32),
            pltpu.VMEM((tokens, width), jnp.bfloat16),
            pltpu.VMEM((tokens, width), jnp.bfloat16),
            pltpu.VMEM((half, width), jnp.bfloat16),
            pltpu.VMEM((half, width), jnp.bfloat16),
            pltpu.SemaphoreType.DMA((5,)),
            pltpu.SemaphoreType.DMA((5,)),
        ],
        compiler_params=pltpu.CompilerParams(
            collective_id=2, has_side_effects=True, vmem_limit_bytes=48 * 1024 * 1024
        ),
    )(attended, out_rows).reshape(2, tokens, width)


def contract_rows(left, right):
    return lax.dot_general(
        left, right, (((0,), (0,)), ((), ())), preferred_element_type=jnp.float32
    )


def middle_kernel(
    scalar_ref, hidden_ref, sum_ref, mods_ref, final_ref, latent_ref, noise_ref, attended_ref,
    next_ref, density_ref, parts_ref, normed_ref, readout_ref, grad_ref,
):
    spread, step_size, drift_velocity, drift_latent, sample_weight, level = (
        scalar_ref[k] for k in range(6)
    )
    passes, tokens, _ = hidden_ref.shape
    inverses, velocity = [], []
    for which in range(passes):
        updated = hidden_ref[which].astype(jnp.float32) + mods_ref[which, 2:3] * sum_ref[
            which
        ].astype(jnp.float32)
        normed, inverse = layer_norm(updated)
        normed_ref[which] = normed
        inverses.append(inverse)
        readout = (normed * (1.0 + mods_ref[which, 4:5]) + mods_ref[which, 3:4]).astype(
            jnp.bfloat16
        )
        readout_ref[which * tokens : (which + 1) * tokens] = readout
        velocity.append(jnp.dot(readout, final_ref[...], preferred_element_type=jnp.float32))
    guided = velocity[1] + guidance * (velocity[0] - velocity[1])
    latent = latent_ref[...]
    centre = latent - step_size * (drift_velocity * guided + drift_latent * latent)
    following = centre + spread * noise_ref[...]
    offset = following - centre
    next_ref[...] = following
    density_ref[0] = jnp.mean(-offset * offset / (2.0 * spread * spread)) - level
    slope = step_size * drift_velocity * offset / (spread * spread * offset.size)
    upstream = sample_weight * slope
    grads = [
        (factor * upstream).astype(jnp.bfloat16) for factor in (guidance, 1.0 - guidance)
    ]
    for which in range(passes):
        readout_grad = lax.dot_general(
            grads[which], final_ref[...], (((1,), (1,)), ((), ())),
            preferred_element_type=jnp.float32,
        )
        updated_grad = layer_norm_back(
            readout_grad * (1.0 + mods_ref[which, 4:5]), normed_ref[which], inverses[which]
        )
        grad_ref[which * tokens : (which + 1) * tokens] = (
            mods_ref[which, 2:3] * updated_grad
        ).astype(jnp.bfloat16)
    columns = attended_ref.shape[1]
    parts_ref[:, :columns] = contract_rows(grad_ref[...], attended_ref[...]).astype(jnp.bfloat16)
    parts_ref[:, columns:] = contract_rows(
        readout_ref[...], jnp.concatenate(grads, 0)
    ).astype(jnp.bfloat16)


def middle(scalars, hidden, total, mods, final_rows, latent, noise, attended):
    passes, tokens, model_width = hidden.shape
    whole = pl.BlockSpec(memory_space=pltpu.VMEM)
    return pl.pallas_call(
        middle_kernel,
        out_shape=(
            jax.ShapeDtypeStruct(latent.shape, jnp.float32),
            jax.ShapeDtypeStruct((1,), jnp.float32),
            jax.ShapeDtypeStruct(
                (model_width, attended.shape[1] + final_rows.shape[1]), jnp.bfloat16
            ),
        ),
        in_specs=[pl.BlockSpec(memory_space=pltpu.SMEM)] + [whole] * 7,
        out_specs=(whole, pl.BlockSpec(memory_space=pltpu.SMEM), whole),
        scratch_shapes=[
            pltpu.VMEM((passes, tokens, model_width), jnp.float32),
            pltpu.VMEM((passes * tokens, model_width), jnp.bfloat16),
            pltpu.VMEM((passes * tokens, model_width), jnp.bfloat16),
        ],
        compiler_params=pltpu.CompilerParams(vmem_limit_bytes=48 * 1024 * 1024),
    )(scalars, hidden, total, mods, final_rows, latent, noise, attended)


def local(
    hidden, text_kv, mods, latents, noise, step_index, group_id, advantages, w_qkv, w_out, w_final
):
    row_count = hidden.shape[2]
    model_width = hidden.shape[3]
    head_columns = text_kv.shape[3] * text_kv.shape[4] // 2
    residual = hidden[0].astype(jnp.float32)
    mod_values = mods[0].astype(jnp.float32)
    normed, inverse = layer_norm(residual)
    modulated = (normed * (1.0 + mod_values[:, 1:2]) + mod_values[:, 0:1]).astype(jnp.bfloat16)
    stacked = modulated.reshape(2 * row_count, model_width)
    dp_size, line_size = lax.axis_size("dp"), lax.axis_size("fsdp")
    blocks = jnp.swapaxes(w_qkv, 0, 1)
    patch = w_final.shape[1]
    group_column = jnp.broadcast_to(
        group_id[:, None].astype(jnp.bfloat16), (w_final.shape[0], patch)
    )
    thin = jnp.concatenate([w_final, group_column], 1)
    gathered, out_rows, all_thin = gather_rows(blocks, w_out, thin, dp_size, line_size)
    gathered = gathered.reshape(3, model_width, head_columns)
    groups = all_thin[:, 0, patch].astype(jnp.int32)
    final_rows = all_thin.reshape(model_width, -1)[:, :patch]
    out_rows = out_rows.reshape(model_width, head_columns)
    attended_flat = attend(stacked, gathered, text_kv[0])
    total = head_sum(attended_flat, out_rows)
    time_now, step_size, noise_scale = plan(step_index[0], STEPS)
    spread = noise_scale * jnp.sqrt(step_size)
    drift_velocity = 1.0 + noise_scale * noise_scale * (1.0 - time_now) / (2.0 * time_now)
    drift_latent = noise_scale * noise_scale / (2.0 * time_now)
    members = jnp.sum((groups == group_id[0]).astype(jnp.float32))
    sample_weight = loss_scale * advantages[0] / members
    level = jnp.log(spread) + 0.5 * math.log(2.0 * math.pi)
    scalars = jnp.stack([spread, step_size, drift_velocity, drift_latent, sample_weight, level])
    following, log_density, parts = middle(
        scalars, hidden[0], total, mod_values, final_rows, latents[0], noise[0],
        attended_flat.reshape(2 * row_count, head_columns),
    )
    grad_out, grad_final = scatter_rows(
        parts.reshape(dp_size * line_size, -1, parts.shape[1]), head_columns, dp_size, line_size
    )
    return (following[None], log_density, grad_out, grad_final)


def solution(mesh):
    in_specs = (
        P(("dp", "fsdp"), None, None, None),
        P(("dp", "fsdp"), None, None, "tp", None),
        P(("dp", "fsdp"), None, None, None),
        P(("dp", "fsdp"), None, None),
        P(("dp", "fsdp"), None, None),
        P(("dp", "fsdp")),
        P(("dp", "fsdp")),
        P(("dp", "fsdp")),
        P(("dp", "fsdp"), None, "tp"),
        P(("dp", "fsdp"), "tp"),
        P(("dp", "fsdp"), None),
    )
    out_specs = (
        P(("dp", "fsdp"), None, None),
        P(("dp", "fsdp")),
        P(("dp", "fsdp"), "tp"),
        P(("dp", "fsdp"), None),
    )
    return jax.shard_map(local, mesh=mesh, in_specs=in_specs, out_specs=out_specs, check_vma=False)
```
